32 devices in a mesh: gx: 4 (over z), gy: 2 (over x), gz: 4 (over y, core).
Axes of the slice: x: 2, y: 2, z: 4, core: 2. Of those that a mesh axis runs over, the one named last changes fastest.
Arguments:
- inputs: bfloat16 [1024, 12288], P('gx', 'gz'), may hold values from -6 to 6
- weight: bfloat16 [12288, 24576], P(('gz', 'gx'), 'gy'), may hold values from -0.0546875 to 0.0546875
- grad_out: bfloat16 [1024, 24576], P(('gx', 'gz'), 'gy'), may hold values from -6 to 6
- pre_act: bfloat16 [1024, 24576], P(('gx', 'gz'), 'gy'), may hold values from -6 to 6
Outputs:
- grad_in: bfloat16 [1024, 12288], P('gx', 'gz')
- grad_weight: bfloat16 [12288, 24576], P(('gz', 'gx'), 'gy')
The draws below stay inside these ranges and needn't reach their ends.
All inputs are finite; a program needn't handle non-finite values.
Results may differ from the reference program's by a relative error of at most 0.0049.
Values may be sent and summed in bfloat16 or wider, within the bound.
A program may use at most 128 MiB of HBM per device.

```python
import jax
import jax.numpy as jnp

D = 12288
FF = 24576
TOKENS = 1024


def level_of(rng, shape, split, smallest, high):
    factor_of = 1.0
    for dim, blocks in split:
        draws = jax.random.uniform(jax.random.fold_in(jax.random.fold_in(rng, 6), dim), (blocks,), jnp.float32, smallest / len(split), high / len(split))
        factor_of = factor_of * jnp.repeat(jnp.exp(draws), shape[dim] // blocks).reshape((-1,) + (1,) * (len(shape) - 1 - dim))
    return factor_of


def normal_values(key, shape, spread, limit, split=(), held_as=jnp.bfloat16):
    loudness = level_of(key, shape, split, -0.22, 0.18) if split else 1.0
    entries = jax.random.normal(key, shape, jnp.float32) * spread * loudness
    return jnp.minimum(jnp.maximum(entries, -limit), limit).astype(held_as)


def setup_inputs(seed: int = 0) -> dict:
    keys = jax.random.split(jax.random.key(seed), 5)
    inputs = normal_values(keys[0], (TOKENS, D), 1.0, 6.0, ((0, 4), (1, 4)))
    weight = normal_values(keys[1], (D, FF), D ** -0.5, 0.0546875, ((0, 16), (1, 2)))
    grad_out = normal_values(keys[2], (TOKENS, FF), 1.0, 6.0, ((0, 16), (1, 2)))
    pre_act = normal_values(keys[3], (TOKENS, FF), 1.0, 6.0, ((0, 16), (1, 2)))
    return {"inputs": inputs, "weight": weight, "grad_out": grad_out, "pre_act": pre_act}


def gelu_slope(value):
    scale = 0.7978845608028654
    tangent = jnp.tanh(scale * (value + 0.044715 * value * value * value))
    inner = scale * (1.0 + 3.0 * 0.044715 * value * value)
    return 0.5 * (1.0 + tangent) + 0.5 * value * (1.0 - tangent * tangent) * inner


def reference(inputs, weight, grad_out, pre_act):
    grad_hidden = (grad_out.astype(jnp.float32) * gelu_slope(pre_act.astype(jnp.float32))).astype(jnp.bfloat16)
    grad_in = jnp.dot(grad_hidden, weight.T, preferred_element_type=jnp.float32).astype(jnp.bfloat16)
    grad_weight = jnp.dot(inputs.T, grad_hidden, preferred_element_type=jnp.float32).astype(jnp.bfloat16)
    return grad_in, grad_weight
```

```python
import functools

import jax
import jax.numpy as jnp
from jax import lax
from jax.experimental import pallas as pl
from jax.experimental.pallas import tpu as pltpu
from jax.sharding import PartitionSpec as P

MESH = pl.DeviceIdType.MESH
F32 = jnp.float32
BF16 = jnp.bfloat16
UP, DOWN, ACROSS, TWIN = 0, 1, 2, 3


def gelu_slope(value):
    scale = 0.7978845608028654
    tangent = jnp.tanh(scale * (value + 0.044715 * value * value * value))
    inner = scale * (1.0 + 3.0 * 0.044715 * value * value)
    return 0.5 * (1.0 + tangent) + 0.5 * value * (1.0 - tangent * tangent) * inner


def kernel(
    nz, chunks,
    go, pa, x_hbm, w_hbm,
    gi_out, gw_out,
    gh, w, xs, xt, acc, psend, precv, osend, gin, stage,
    ring_send, ring_recv, x_send, x_recv, p_send, p_recv, o_send, o_recv, w_sem, gw_sem, gi_sem,
):
    z, x, q = lax.axis_index("gx"), lax.axis_index("gy"), lax.axis_index("gz")
    rows = go.shape[0]
    group = 4 * rows
    half = group // 2
    hidden = gh.shape[1]
    wide = hidden // chunks
    depth = w.shape[0]
    twin = q + 1 - 2 * lax.rem(q, 2)
    across = lax.rem(q + 2, 4)
    diagonal = lax.rem(twin + 2, 4)

    def at(zz, xx, qq):
        return (zz, xx, qq)

    barrier = pltpu.get_barrier_semaphore()
    for k in range(1, nz):
        for xx in (x, 1 - x):
            pl.semaphore_signal(
                barrier, inc=1, device_id=at(lax.rem(z + k, nz), xx, q), device_id_type=MESH
            )
    for partner in (at(z, 1 - x, q), at(z, x, twin), at(z, x, across)):
        pl.semaphore_signal(barrier, inc=1, device_id=partner, device_id_type=MESH)

    w_copy = pltpu.make_async_copy(w_hbm, w, w_sem)
    w_copy.start()

    def columns(c):
        return pl.ds(pl.multiple_of(c * wide, wide), wide)

    def block(zz, qq, cols):
        return gh.at[pl.ds(pl.multiple_of(zz * group + qq * rows, rows), rows), cols]

    def partner(kind):
        return (at(z + 1, x, q), at(z - 1, x, q), at(z, x, across), at(z, x, twin))[kind]

    def move(kind, zz, qq, cols, c):
        return pltpu.make_async_remote_copy(
            src_ref=block(zz, qq, cols),
            dst_ref=block(zz, qq, cols),
            send_sem=ring_send.at[kind, zz, qq],
            recv_sem=ring_recv.at[zz, qq, c],
            device_id=partner(kind),
            device_id_type=MESH,
        )

    def send(kind, zz, qq, c):
        move(kind, zz, qq, columns(c), c).start()

    def arrived(zz, qq, c):
        move(TWIN, zz, qq, columns(c), c).wait_recv()

    def up_or_down(kind, zz, c):
        if kind == UP:
            pl.when(z < nz - 1)(lambda: send(UP, zz, q, c))
        else:
            pl.when(z > 0)(lambda: send(DOWN, zz, q, c))

    narrow = min(256, wide)

    def make_own(c, _):
        def piece(i, _):
            cols = pl.ds(pl.multiple_of(c * wide + i * narrow, narrow), narrow)
            value = go[:, cols].astype(F32) * gelu_slope(pa[:, cols].astype(F32))
            block(z, q, cols)[...] = value.astype(BF16)
            return 0

        lax.fori_loop(0, wide // narrow, piece, 0)

        @pl.when(c == 0)
        def _():
            pl.semaphore_wait(barrier, 2 * (nz - 1) + 3)

        up_or_down(UP, z, c)
        up_or_down(DOWN, z, c)
        send(ACROSS, z, q, c)
        send(TWIN, z, q, c)
        return 0

    lax.fori_loop(0, chunks, make_own, 0)
    w_copy.wait()

    def x_move(zt, zs):
        return pltpu.make_async_remote_copy(
            src_ref=x_hbm.at[:, pl.ds(pl.multiple_of(zt * depth, depth), depth)],
            dst_ref=xs.at[pl.ds(pl.multiple_of(zs * group, group), group), :],
            send_sem=x_send.at[zt],
            recv_sem=x_recv.at[zs],
            device_id=at(zt, x, q),
            device_id_type=MESH,
        )

    own_x = pltpu.make_async_copy(
        x_hbm.at[:, pl.ds(pl.multiple_of(z * depth, depth), depth)],
        xs.at[pl.ds(pl.multiple_of(z * group, group), group), :],
        x_recv.at[z],
    )

    def sources(j):
        if j == 0:
            return [(0, z, None)]
        return [(0, z - j, z >= j), (1, z + j, z + j < nz)]

    def when(condition, body):
        if condition is None:
            body()
        else:
            pl.when(condition)(body)

    tile = min(256, depth)

    def add_input(slot, zz, c):
        tokens = pl.ds(pl.multiple_of(zz * group, group), group)

        def piece(i, _):
            out = pl.ds(pl.multiple_of(i * tile, tile), tile)
            part = lax.dot_general(
                gh[tokens, columns(c)], w[out, columns(c)],
                (((1,), (1,)), ((), ())), preferred_element_type=F32,
            )

            @pl.when(c == 0)
            def _():
                acc[slot, :, out] = part

            @pl.when(c > 0)
            def _():
                acc[slot, :, out] += part

            return 0

        lax.fori_loop(0, depth // tile, piece, 0)

    def p_move(zz):
        return pltpu.make_async_remote_copy(
            src_ref=psend.at[zz],
            dst_ref=precv.at[zz],
            send_sem=p_send.at[zz],
            recv_sem=p_recv.at[zz],
            device_id=at(z, 1 - x, q),
            device_id_type=MESH,
        )

    def o_dst(zs, xx):
        return gin.at[
            pl.ds(pl.multiple_of(xx * half, half), half),
            pl.ds(pl.multiple_of(zs * depth, depth), depth),
        ]

    def o_move(zz, xt_, xs_, zs):
        return pltpu.make_async_remote_copy(
            src_ref=osend.at[zz],
            dst_ref=o_dst(zs, xs_),
            send_sem=o_send.at[zz, xt_],
            recv_sem=o_recv.at[zs, xs_],
            device_id=at(zz, xt_, q),
            device_id_type=MESH,
        )

    def exchange(slot, zz):
        theirs = pl.ds(pl.multiple_of((1 - x) * half, half), half)
        psend[zz] = acc[slot, theirs, :].astype(BF16)
        p_move(zz).start()

    def finish(slot, zz, own):
        ours = pl.ds(pl.multiple_of(x * half, half), half)
        p_move(zz).wait()
        osend[zz] = (acc[slot, ours, :] + precv[zz].astype(F32)).astype(BF16)
        if own:
            o_dst(z, x)[...] = osend[zz]
            o_move(zz, 1 - x, x, z).start()
        else:
            o_move(zz, x, x, z).start()
            o_move(zz, 1 - x, x, z).start()

    for j in range(nz):
        last = j == nz - 1
        if j == 1:
            own_x.start()
            for k in range(1, nz):
                x_move(lax.rem(z + k, nz), z).start()
        if last:
            own_x.wait()
            for k in range(1, nz):
                x_move(z, lax.rem(z + k, nz)).wait_recv()
            for k in range(xs.shape[0] // group):
                part = pl.ds(k * group, group)
                xt[:, part] = xs[part, :].T

        def step(c, _):
            if not last:
                for (_, zz, there), kind in zip(sources(j + 1), (UP, DOWN)):

                    def pass_on(zz=zz, kind=kind):
                        arrived(zz, q, c)
                        up_or_down(kind, zz, c)
                        send(ACROSS, zz, q, c)
                        send(TWIN, zz, q, c)

                    when(there, pass_on)
            for slot, zz, there in sources(j):

                def over(zz=zz):
                    arrived(zz, across, c)
                    send(TWIN, zz, across, c)

                when(there, over)

            if j > 0:
                @pl.when(c == 0)
                def _():
                    for slot, zz, there in sources(j - 1):
                        when(there, functools.partial(finish, slot, zz, j == 1))

            for slot, zz, there in sources(j):

                def use(slot=slot, zz=zz):
                    arrived(zz, twin, c)
                    arrived(zz, diagonal, c)
                    add_input(slot, zz, c)

                when(there, use)

            @pl.when(c == chunks - 1)
            def _():
                for slot, zz, there in sources(j):
                    when(there, functools.partial(exchange, slot, zz))

            if last:
                turn = lax.rem(c, 2)

                def out_copy(cc):
                    return pltpu.make_async_copy(
                        stage.at[turn], gw_out.at[:, columns(cc)], gw_sem.at[turn]
                    )

                @pl.when(c >= 2)
                def _():
                    out_copy(c - 2).wait()

                def piece(i, _):
                    here = pl.ds(pl.multiple_of(i * narrow, narrow), narrow)
                    there = pl.ds(pl.multiple_of(c * wide + i * narrow, narrow), narrow)
                    stage[turn, :, here] = jnp.dot(
                        xt[...], gh[:, there], preferred_element_type=F32
                    ).astype(BF16)
                    return 0

                lax.fori_loop(0, wide // narrow, piece, 0)
                out_copy(c).start()
            return 0

        lax.fori_loop(0, chunks, step, 0)

    for slot, zz, there in sources(nz - 1):
        when(there, functools.partial(finish, slot, zz, nz == 1))

    for k in range(nz):
        zs = lax.rem(z + k, nz)
        for xx in (x, 1 - x):
            if k == 0:
                continue
            o_move(zs, xx, xx, zs).wait_recv()
            o_move(zs, xx, x, z).wait_send()
    o_move(z, 1 - x, 1 - x, z).wait_recv()
    o_move(z, 1 - x, x, z).wait_send()
    gi_copy = pltpu.make_async_copy(gin, gi_out, gi_sem)
    gi_copy.start()
    for k in range(1, nz):
        x_move(lax.rem(z + k, nz), z).wait_send()
    everything = pl.ds(0, hidden)
    for zz in range(nz):
        for there, kind in (((z < nz - 1) & (z >= zz), UP), ((z > 0) & (z <= zz), DOWN)):
            pl.when(there)(
                lambda kind=kind, zz=zz: move(kind, zz, q, everything, 0).wait_send()
            )
        move(ACROSS, zz, q, everything, 0).wait_send()
        move(TWIN, zz, q, everything, 0).wait_send()
        move(TWIN, zz, across, everything, 0).wait_send()
    for c in range(max(chunks - 2, 0), chunks):
        pltpu.make_async_copy(
            stage.at[c % 2], gw_out.at[:, pl.ds(c * wide, wide)], gw_sem.at[c % 2]
        ).wait()
    gi_copy.wait()


def fused(nz, inputs, weight, grad_out, pre_act):
    group, model = inputs.shape
    depth, hidden = weight.shape
    rows = grad_out.shape[0]
    tokens = nz * group
    chunks = 12
    wide = hidden // chunks
    half = group // 2
    vmem = pl.BlockSpec(memory_space=pltpu.VMEM)
    hbm = pl.BlockSpec(memory_space=pl.ANY)
    dma = pltpu.SemaphoreType.DMA
    return pl.pallas_call(
        functools.partial(kernel, nz, chunks),
        out_shape=(
            jax.ShapeDtypeStruct((group, model), BF16),
            jax.ShapeDtypeStruct((depth, hidden), BF16),
        ),
        in_specs=[vmem, vmem, hbm, hbm],
        out_specs=(hbm, hbm),
        scratch_shapes=[
            pltpu.VMEM((tokens, hidden), BF16),
            pltpu.VMEM((depth, hidden), BF16),
            pltpu.VMEM((tokens, depth), BF16),
            pltpu.VMEM((depth, tokens), BF16),
            pltpu.VMEM((2, group, depth), F32),
            pltpu.VMEM((nz, half, depth), BF16),
            pltpu.VMEM((nz, half, depth), BF16),
            pltpu.VMEM((nz, half, depth), BF16),
            pltpu.VMEM((group, model), BF16),
            pltpu.VMEM((2, depth, wide), BF16),
            dma((4, nz, 4)),
            dma((nz, 4, chunks)),
            dma((nz,)),
            dma((nz,)),
            dma((nz,)),
            dma((nz,)),
            dma((nz, 2)),
            dma((nz, 2)),
            dma(()),
            dma((2,)),
            dma(()),
        ],
        compiler_params=pltpu.CompilerParams(
            collective_id=0, has_side_effects=True, vmem_limit_bytes=62 * 1024 * 1024
        ),
        cost_estimate=pl.CostEstimate(
            flops=4 * tokens * depth * hidden,
            bytes_accessed=4 * depth * hidden,
            transcendentals=rows * hidden,
        ),
    )(grad_out, pre_act, inputs, weight)


def plain(inputs, weight, grad_out, pre_act):
    grad_hidden = (grad_out.astype(F32) * gelu_slope(pre_act.astype(F32))).astype(BF16)
    input_cols = lax.all_to_all(inputs, "gx", split_axis=1, concat_axis=0, tiled=True)
    piece = lax.all_gather(grad_hidden, ("gx", "gz"), axis=0, tiled=True)
    weight_sum = lax.dot_general(
        input_cols, piece, (((0,), (0,)), ((), ())), preferred_element_type=F32
    )
    product = lax.dot_general(
        piece, weight, (((1,), (1,)), ((), ())), preferred_element_type=F32
    )
    summed = lax.psum(product, "gy").astype(BF16)
    grad_in = lax.all_to_all(summed, "gx", split_axis=0, concat_axis=1, tiled=True)
    return (grad_in, weight_sum.astype(BF16))


def solution(mesh):
    in_specs = (P("gx", "gz"), P(("gz", "gx"), "gy"), P(("gx", "gz"), "gy"), P(("gx", "gz"), "gy"))
    out_specs = (P("gx", "gz"), P(("gz", "gx"), "gy"))
    if mesh.shape["gy"] == 2 and mesh.shape["gz"] == 4 and mesh.shape["gx"] > 1:
        shards = functools.partial(fused, mesh.shape["gx"])
    else:
        shards = plain
    return jax.shard_map(shards, mesh=mesh, in_specs=in_specs, out_specs=out_specs, check_vma=False)
```

```python
import functools

import jax
import jax.numpy as jnp
from jax import lax
from jax.experimental import pallas as pl
from jax.experimental.pallas import tpu as pltpu
from jax.sharding import PartitionSpec as P

MESH = pl.DeviceIdType.MESH
F32 = jnp.float32
BF16 = jnp.bfloat16
UP, DOWN, ACROSS, TWIN = 0, 1, 2, 3


def gelu_slope(value):
    scale = 0.7978845608028654
    tangent = jnp.tanh(scale * (value + 0.044715 * value * value * value))
    inner = scale * (1.0 + 3.0 * 0.044715 * value * value)
    return 0.5 * (1.0 + tangent) + 0.5 * value * (1.0 - tangent * tangent) * inner


def kernel(
    nz, chunks,
    go, pa, x_hbm, w_hbm,
    gi_out, gw_out,
    gh, w, xs, xt, acc, psend, precv, osend, gin, stage,
    ring_send, ring_recv, x_send, x_recv, p_send, p_recv, o_send, o_recv, w_sem, gw_sem, gi_sem,
):
    z, x, q = lax.axis_index("gx"), lax.axis_index("gy"), lax.axis_index("gz")
    rows = go.shape[0]
    group = 4 * rows
    half = group // 2
    hidden = gh.shape[1]
    wide = hidden // chunks
    depth = w.shape[0]
    twin = q + 1 - 2 * lax.rem(q, 2)
    across = lax.rem(q + 2, 4)
    diagonal = lax.rem(twin + 2, 4)

    def at(zz, xx, qq):
        return (zz, xx, qq)

    barrier = pltpu.get_barrier_semaphore()
    for k in range(1, nz):
        for xx in (x, 1 - x):
            pl.semaphore_signal(
                barrier, inc=1, device_id=at(lax.rem(z + k, nz), xx, q), device_id_type=MESH
            )
    for partner in (at(z, 1 - x, q), at(z, x, twin), at(z, x, across)):
        pl.semaphore_signal(barrier, inc=1, device_id=partner, device_id_type=MESH)

    w_copy = pltpu.make_async_copy(w_hbm, w, w_sem)
    w_copy.start()

    def columns(c):
        return pl.ds(pl.multiple_of(c * wide, wide), wide)

    def block(zz, qq, cols):
        return gh.at[pl.ds(pl.multiple_of(zz * group + qq * rows, rows), rows), cols]

    def partner(kind):
        return (at(z + 1, x, q), at(z - 1, x, q), at(z, x, across), at(z, x, twin))[kind]

    def move(kind, zz, qq, cols, c):
        return pltpu.make_async_remote_copy(
            src_ref=block(zz, qq, cols),
            dst_ref=block(zz, qq, cols),
            send_sem=ring_send.at[kind, zz, qq],
            recv_sem=ring_recv.at[zz, qq, c],
            device_id=partner(kind),
            device_id_type=MESH,
        )

    def send(kind, zz, qq, c):
        move(kind, zz, qq, columns(c), c).start()

    def arrived(zz, qq, c):
        move(TWIN, zz, qq, columns(c), c).wait_recv()

    def up_or_down(kind, zz, c):
        if kind == UP:
            pl.when(z < nz - 1)(lambda: send(UP, zz, q, c))
        else:
            pl.when(z > 0)(lambda: send(DOWN, zz, q, c))

    narrow = min(256, wide)

    def make_own(c, _):
        def piece(i, _):
            cols = pl.ds(pl.multiple_of(c * wide + i * narrow, narrow), narrow)
            value = go[:, cols].astype(F32) * gelu_slope(pa[:, cols].astype(F32))
            block(z, q, cols)[...] = value.astype(BF16)
            return 0

        lax.fori_loop(0, wide // narrow, piece, 0)

        @pl.when(c == 0)
        def _():
            pl.semaphore_wait(barrier, 2 * (nz - 1) + 3)

        up_or_down(UP, z, c)
        up_or_down(DOWN, z, c)
        send(ACROSS, z, q, c)
        send(TWIN, z, q, c)
        return 0

    lax.fori_loop(0, chunks, make_own, 0)
    w_copy.wait()

    def x_rows(zs, xx):
        return xs.at[pl.ds(pl.multiple_of(zs * group + xx * half, half), half), :]

    def x_move(zt, zs):
        return pltpu.make_async_remote_copy(
            src_ref=x_hbm.at[
                pl.ds(pl.multiple_of(x * half, half), half),
                pl.ds(pl.multiple_of(zt * depth, depth), depth),
            ],
            dst_ref=x_rows(zs, x),
            send_sem=x_send.at[zt, 0],
            recv_sem=x_recv.at[zs, x],
            device_id=at(zt, x, q),
            device_id_type=MESH,
        )

    def x_share(zs, xx):
        return pltpu.make_async_remote_copy(
            src_ref=x_rows(zs, xx),
            dst_ref=x_rows(zs, xx),
            send_sem=x_send.at[zs, 1],
            recv_sem=x_recv.at[zs, xx],
            device_id=at(z, 1 - x, q),
            device_id_type=MESH,
        )

    own_x = pltpu.make_async_copy(
        x_hbm.at[:, pl.ds(pl.multiple_of(z * depth, depth), depth)],
        xs.at[pl.ds(pl.multiple_of(z * group, group), group), :],
        x_recv.at[z, 0],
    )

    def sources(j):
        if j == 0:
            return [(0, z, None)]
        first = 2 * (j % 2)
        return [(first, z - j, z >= j), (first + 1, z + j, z + j < nz)]

    def when(condition, body):
        if condition is None:
            body()
        else:
            pl.when(condition)(body)

    tile = min(256, depth)

    def add_input(slot, zz, c):
        tokens = pl.ds(pl.multiple_of(zz * group, group), group)

        def piece(i, _):
            out = pl.ds(pl.multiple_of(i * tile, tile), tile)
            part = lax.dot_general(
                gh[tokens, columns(c)], w[out, columns(c)],
                (((1,), (1,)), ((), ())), preferred_element_type=F32,
            )

            @pl.when(c == 0)
            def _():
                acc[slot, :, out] = part

            @pl.when(c > 0)
            def _():
                acc[slot, :, out] += part

            return 0

        lax.fori_loop(0, depth // tile, piece, 0)

    def p_move(zz):
        return pltpu.make_async_remote_copy(
            src_ref=psend.at[zz],
            dst_ref=precv.at[zz],
            send_sem=p_send.at[zz],
            recv_sem=p_recv.at[zz],
            device_id=at(z, 1 - x, q),
            device_id_type=MESH,
        )

    def o_dst(zs, xx):
        return gin.at[
            pl.ds(pl.multiple_of(xx * half, half), half),
            pl.ds(pl.multiple_of(zs * depth, depth), depth),
        ]

    def o_move(zt, zs):
        return pltpu.make_async_remote_copy(
            src_ref=osend.at[zt],
            dst_ref=o_dst(zs, x),
            send_sem=o_send.at[zt, 0],
            recv_sem=o_recv.at[zs, x],
            device_id=at(zt, x, q),
            device_id_type=MESH,
        )

    def o_share(zs, xx):
        return pltpu.make_async_remote_copy(
            src_ref=o_dst(zs, xx),
            dst_ref=o_dst(zs, xx),
            send_sem=o_send.at[zs, 1],
            recv_sem=o_recv.at[zs, xx],
            device_id=at(z, 1 - x, q),
            device_id_type=MESH,
        )

    def share_from(distance):
        for zs, there in ((z - distance, z >= distance), (z + distance, z + distance < nz)):

            def pass_over(zs=zs):
                o_move(z, zs).wait_recv()
                o_share(zs, x).start()

            pl.when(there)(pass_over)

    def exchange(slot, zz):
        theirs = pl.ds(pl.multiple_of((1 - x) * half, half), half)
        psend[zz] = acc[slot, theirs, :].astype(BF16)
        p_move(zz).start()

    def finish(slot, zz, own):
        ours = pl.ds(pl.multiple_of(x * half, half), half)
        p_move(zz).wait()
        osend[zz] = (acc[slot, ours, :] + precv[zz].astype(F32)).astype(BF16)
        if own:
            o_dst(z, x)[...] = osend[zz]
            o_share(z, x).start()
        else:
            o_move(zz, z).start()

    for j in range(nz):
        last = j == nz - 1
        if j == 1:
            own_x.start()
            for k in range(1, nz):
                x_move(lax.rem(z + k, nz), z).start()
        if j == max(nz - 2, 1):
            for k in range(1, nz):
                x_move(z, lax.rem(z + k, nz)).wait_recv()
                x_share(lax.rem(z + k, nz), x).start()
        if last:
            own_x.wait()
            for k in range(1, nz):
                x_share(lax.rem(z + k, nz), 1 - x).wait_recv()
            for k in range(xs.shape[0] // group):
                part = pl.ds(k * group, group)
                xt[:, part] = xs[part, :].T

        def step(c, _):
            if not last:
                for (_, zz, there), kind in zip(sources(j + 1), (UP, DOWN)):

                    def pass_on(zz=zz, kind=kind):
                        arrived(zz, q, c)
                        up_or_down(kind, zz, c)
                        send(ACROSS, zz, q, c)
                        send(TWIN, zz, q, c)

                    when(there, pass_on)
            for slot, zz, there in sources(j):

                def over(zz=zz):
                    arrived(zz, across, c)
                    send(TWIN, zz, across, c)

                when(there, over)

            if j > 0:
                @pl.when(c == 2)
                def _():
                    for slot, zz, there in sources(j - 1):
                        when(there, functools.partial(finish, slot, zz, j == 1))

            for slot, zz, there in sources(j):

                def use(slot=slot, zz=zz):
                    arrived(zz, twin, c)
                    arrived(zz, diagonal, c)
                    add_input(slot, zz, c)

                when(there, use)

            @pl.when(c == chunks - 1)
            def _():
                for slot, zz, there in sources(j):
                    when(there, functools.partial(exchange, slot, zz))

            if last:
                for distance in range(1, nz - 1):
                    pl.when(c == chunks - 1 - 2 * (nz - 2 - distance))(
                        functools.partial(share_from, distance)
                    )

                turn = lax.rem(c, 2)

                def out_copy(cc):
                    return pltpu.make_async_copy(
                        stage.at[turn], gw_out.at[:, columns(cc)], gw_sem.at[turn]
                    )

                @pl.when(c >= 2)
                def _():
                    out_copy(c - 2).wait()

                def piece(i, _):
                    here = pl.ds(pl.multiple_of(i * narrow, narrow), narrow)
                    there = pl.ds(pl.multiple_of(c * wide + i * narrow, narrow), narrow)
                    stage[turn, :, here] = jnp.dot(
                        xt[...], gh[:, there], preferred_element_type=F32
                    ).astype(BF16)
                    return 0

                lax.fori_loop(0, wide // narrow, piece, 0)
                out_copy(c).start()
            return 0

        lax.fori_loop(0, chunks, step, 0)

    for slot, zz, there in sources(nz - 1):
        when(there, functools.partial(finish, slot, zz, nz == 1))

    share_from(nz - 1)
    for k in range(nz):
        zs = lax.rem(z + k, nz)
        o_share(zs, 1 - x).wait_recv()
        o_share(zs, x).wait_send()
        if k > 0:
            o_move(zs, z).wait_send()
    gi_copy = pltpu.make_async_copy(gin, gi_out, gi_sem)
    gi_copy.start()
    for k in range(1, nz):
        x_move(lax.rem(z + k, nz), z).wait_send()
        x_share(lax.rem(z + k, nz), x).wait_send()
    everything = pl.ds(0, hidden)
    for zz in range(nz):
        for there, kind in (((z < nz - 1) & (z >= zz), UP), ((z > 0) & (z <= zz), DOWN)):
            pl.when(there)(
                lambda kind=kind, zz=zz: move(kind, zz, q, everything, 0).wait_send()
            )
        move(ACROSS, zz, q, everything, 0).wait_send()
        move(TWIN, zz, q, everything, 0).wait_send()
        move(TWIN, zz, across, everything, 0).wait_send()
    for c in range(max(chunks - 2, 0), chunks):
        pltpu.make_async_copy(
            stage.at[c % 2], gw_out.at[:, pl.ds(c * wide, wide)], gw_sem.at[c % 2]
        ).wait()
    gi_copy.wait()


def fused(nz, inputs, weight, grad_out, pre_act):
    group, model = inputs.shape
    depth, hidden = weight.shape
    rows = grad_out.shape[0]
    tokens = nz * group
    chunks = 12
    wide = hidden // chunks
    half = group // 2
    vmem = pl.BlockSpec(memory_space=pltpu.VMEM)
    hbm = pl.BlockSpec(memory_space=pl.ANY)
    dma = pltpu.SemaphoreType.DMA
    return pl.pallas_call(
        functools.partial(kernel, nz, chunks),
        out_shape=(
            jax.ShapeDtypeStruct((group, model), BF16),
            jax.ShapeDtypeStruct((depth, hidden), BF16),
        ),
        in_specs=[vmem, vmem, hbm, hbm],
        out_specs=(hbm, hbm),
        scratch_shapes=[
            pltpu.VMEM((tokens, hidden), BF16),
            pltpu.VMEM((depth, hidden), BF16),
            pltpu.VMEM((tokens, depth), BF16),
            pltpu.VMEM((depth, tokens), BF16),
            pltpu.VMEM((4, group, depth), F32),
            pltpu.VMEM((nz, half, depth), BF16),
            pltpu.VMEM((nz, half, depth), BF16),
            pltpu.VMEM((nz, half, depth), BF16),
            pltpu.VMEM((group, model), BF16),
            pltpu.VMEM((2, depth, wide), BF16),
            dma((4, nz, 4)),
            dma((nz, 4, chunks)),
            dma((nz, 2)),
            dma((nz, 2)),
            dma((nz,)),
            dma((nz,)),
            dma((nz, 2)),
            dma((nz, 2)),
            dma(()),
            dma((2,)),
            dma(()),
        ],
        compiler_params=pltpu.CompilerParams(
            collective_id=0, has_side_effects=True, vmem_limit_bytes=62 * 1024 * 1024
        ),
        cost_estimate=pl.CostEstimate(
            flops=4 * tokens * depth * hidden,
            bytes_accessed=4 * depth * hidden,
            transcendentals=rows * hidden,
        ),
    )(grad_out, pre_act, inputs, weight)


def plain(inputs, weight, grad_out, pre_act):
    grad_hidden = (grad_out.astype(F32) * gelu_slope(pre_act.astype(F32))).astype(BF16)
    input_cols = lax.all_to_all(inputs, "gx", split_axis=1, concat_axis=0, tiled=True)
    piece = lax.all_gather(grad_hidden, ("gx", "gz"), axis=0, tiled=True)
    weight_sum = lax.dot_general(
        input_cols, piece, (((0,), (0,)), ((), ())), preferred_element_type=F32
    )
    product = lax.dot_general(
        piece, weight, (((1,), (1,)), ((), ())), preferred_element_type=F32
    )
    summed = lax.psum(product, "gy").astype(BF16)
    grad_in = lax.all_to_all(summed, "gx", split_axis=0, concat_axis=1, tiled=True)
    return (grad_in, weight_sum.astype(BF16))


def solution(mesh):
    in_specs = (P("gx", "gz"), P(("gz", "gx"), "gy"), P(("gx", "gz"), "gy"), P(("gx", "gz"), "gy"))
    out_specs = (P("gx", "gz"), P(("gz", "gx"), "gy"))
    if mesh.shape["gy"] == 2 and mesh.shape["gz"] == 4 and mesh.shape["gx"] > 1:
        shards = functools.partial(fused, mesh.shape["gx"])
    else:
        shards = plain
    return jax.shard_map(shards, mesh=mesh, in_specs=in_specs, out_specs=out_specs, check_vma=False)
```

```python
import functools

import jax
import jax.numpy as jnp
from jax import lax
from jax.experimental import pallas as pl
from jax.experimental.pallas import tpu as pltpu
from jax.sharding import PartitionSpec as P

MESH = pl.DeviceIdType.MESH
F32 = jnp.float32
BF16 = jnp.bfloat16
UP, DOWN, ACROSS, TWIN = 0, 1, 2, 3


def gelu_slope(value):
    scale = 0.7978845608028654
    tangent = jnp.tanh(scale * (value + 0.044715 * value * value * value))
    inner = scale * (1.0 + 3.0 * 0.044715 * value * value)
    return 0.5 * (1.0 + tangent) + 0.5 * value * (1.0 - tangent * tangent) * inner


def kernel(
    nz, chunks,
    go, pa, x_hbm, w_hbm,
    gi_out, gw_out, far_out,
    gh, w, xs, xt, acc, psend, precv, osend, gin, stage,
    ring_send, ring_recv, x_send, x_recv, p_send, p_recv, o_send, o_recv, w_sem, gw_sem, gi_sem, far_sem,
):
    z, x, q = lax.axis_index("gx"), lax.axis_index("gy"), lax.axis_index("gz")
    rows = go.shape[0]
    group = 4 * rows
    half = group // 2
    hidden = gh.shape[1]
    wide = hidden // chunks
    depth = w.shape[0]
    twin = q + 1 - 2 * lax.rem(q, 2)
    across = lax.rem(q + 2, 4)
    diagonal = lax.rem(twin + 2, 4)

    def at(zz, xx, qq):
        return (zz, xx, qq)

    barrier = pltpu.get_barrier_semaphore()
    for k in range(1, nz):
        for xx in (x, 1 - x):
            pl.semaphore_signal(
                barrier, inc=1, device_id=at(lax.rem(z + k, nz), xx, q), device_id_type=MESH
            )
    for partner in (at(z, 1 - x, q), at(z, x, twin), at(z, x, across)):
        pl.semaphore_signal(barrier, inc=1, device_id=partner, device_id_type=MESH)

    w_copy = pltpu.make_async_copy(w_hbm, w, w_sem)
    w_copy.start()

    def columns(c):
        return pl.ds(pl.multiple_of(c * wide, wide), wide)

    def block(zz, qq, cols):
        return gh.at[pl.ds(pl.multiple_of(zz * group + qq * rows, rows), rows), cols]

    def partner(kind):
        return (at(z + 1, x, q), at(z - 1, x, q), at(z, x, across), at(z, x, twin))[kind]

    def move(kind, zz, qq, cols, c):
        return pltpu.make_async_remote_copy(
            src_ref=block(zz, qq, cols),
            dst_ref=block(zz, qq, cols),
            send_sem=ring_send.at[kind, zz, qq],
            recv_sem=ring_recv.at[zz, qq, c],
            device_id=partner(kind),
            device_id_type=MESH,
        )

    def send(kind, zz, qq, c):
        move(kind, zz, qq, columns(c), c).start()

    def arrived(zz, qq, c):
        move(TWIN, zz, qq, columns(c), c).wait_recv()

    def up_or_down(kind, zz, c):
        if kind == UP:
            pl.when(z < nz - 1)(lambda: send(UP, zz, q, c))
        else:
            pl.when(z > 0)(lambda: send(DOWN, zz, q, c))

    narrow = min(256, wide)

    def make_own(c, _):
        def piece(i, _):
            cols = pl.ds(pl.multiple_of(c * wide + i * narrow, narrow), narrow)
            value = go[:, cols].astype(F32) * gelu_slope(pa[:, cols].astype(F32))
            block(z, q, cols)[...] = value.astype(BF16)
            return 0

        lax.fori_loop(0, wide // narrow, piece, 0)

        @pl.when(c == 0)
        def _():
            pl.semaphore_wait(barrier, 2 * (nz - 1) + 3)

        up_or_down(UP, z, c)
        up_or_down(DOWN, z, c)
        send(ACROSS, z, q, c)
        send(TWIN, z, q, c)
        return 0

    lax.fori_loop(0, chunks, make_own, 0)
    w_copy.wait()

    def x_rows(zs, xx):
        return xs.at[pl.ds(pl.multiple_of(zs * group + xx * half, half), half), :]

    def x_move(zt, zs):
        return pltpu.make_async_remote_copy(
            src_ref=x_hbm.at[
                pl.ds(pl.multiple_of(x * half, half), half),
                pl.ds(pl.multiple_of(zt * depth, depth), depth),
            ],
            dst_ref=x_rows(zs, x),
            send_sem=x_send.at[zt, 0],
            recv_sem=x_recv.at[zs, x],
            device_id=at(zt, x, q),
            device_id_type=MESH,
        )

    def x_share(zs, xx):
        return pltpu.make_async_remote_copy(
            src_ref=x_rows(zs, xx),
            dst_ref=x_rows(zs, xx),
            send_sem=x_send.at[zs, 1],
            recv_sem=x_recv.at[zs, xx],
            device_id=at(z, 1 - x, q),
            device_id_type=MESH,
        )

    own_x = pltpu.make_async_copy(
        x_hbm.at[:, pl.ds(pl.multiple_of(z * depth, depth), depth)],
        xs.at[pl.ds(pl.multiple_of(z * group, group), group), :],
        x_recv.at[z, 0],
    )

    def sources(j):
        if j == 0:
            return [(0, z, None)]
        first = 2 * (j % 2)
        return [(first, z - j, z >= j), (first + 1, z + j, z + j < nz)]

    def when(condition, body):
        if condition is None:
            body()
        else:
            pl.when(condition)(body)

    tile = min(256, depth)

    def add_input(slot, zz, c):
        tokens = pl.ds(pl.multiple_of(zz * group, group), group)

        def piece(i, _):
            out = pl.ds(pl.multiple_of(i * tile, tile), tile)
            part = lax.dot_general(
                gh[tokens, columns(c)], w[out, columns(c)],
                (((1,), (1,)), ((), ())), preferred_element_type=F32,
            )

            @pl.when(c == 0)
            def _():
                acc[slot, :, out] = part

            @pl.when(c > 0)
            def _():
                acc[slot, :, out] += part

            return 0

        lax.fori_loop(0, depth // tile, piece, 0)

    def p_move(zz):
        return pltpu.make_async_remote_copy(
            src_ref=psend.at[zz],
            dst_ref=precv.at[zz],
            send_sem=p_send.at[zz],
            recv_sem=p_recv.at[zz],
            device_id=at(z, 1 - x, q),
            device_id_type=MESH,
        )

    def o_dst(zs, xx):
        return gin.at[
            pl.ds(pl.multiple_of(xx * half, half), half),
            pl.ds(pl.multiple_of(zs * depth, depth), depth),
        ]

    def o_move(zt, zs):
        return pltpu.make_async_remote_copy(
            src_ref=osend.at[zt],
            dst_ref=o_dst(zs, x),
            send_sem=o_send.at[zt, 0],
            recv_sem=o_recv.at[zs, x],
            device_id=at(zt, x, q),
            device_id_type=MESH,
        )

    def o_share(zs, xx):
        return pltpu.make_async_remote_copy(
            src_ref=o_dst(zs, xx),
            dst_ref=o_dst(zs, xx),
            send_sem=o_send.at[zs, 1],
            recv_sem=o_recv.at[zs, xx],
            device_id=at(z, 1 - x, q),
            device_id_type=MESH,
        )

    def share_from(distance):
        for zs, there in ((z - distance, z >= distance), (z + distance, z + distance < nz)):

            def pass_over(zs=zs):
                o_move(z, zs).wait_recv()
                o_share(zs, x).start()

            pl.when(there)(pass_over)

    def exchange(slot, zz):
        theirs = pl.ds(pl.multiple_of((1 - x) * half, half), half)
        psend[zz] = acc[slot, theirs, :].astype(BF16)
        p_move(zz).start()

    def finish(slot, zz, own, far):
        ours = pl.ds(pl.multiple_of(x * half, half), half)
        p_move(zz).wait()
        osend[zz] = (acc[slot, ours, :] + precv[zz].astype(F32)).astype(BF16)
        if far:
            for xx in range(2):
                o_dst(zz, xx)[...] = jnp.zeros((half, depth), BF16)
            pltpu.make_async_copy(osend.at[zz], far_out, far_sem).start()
        elif own:
            o_dst(z, x)[...] = osend[zz]
            o_share(z, x).start()
        else:
            o_move(zz, z).start()

    for j in range(nz):
        last = j == nz - 1
        if j == 1:
            own_x.start()
            for k in range(1, nz):
                x_move(lax.rem(z + k, nz), z).start()
        if j == max(nz - 2, 1):
            for k in range(1, nz):
                x_move(z, lax.rem(z + k, nz)).wait_recv()
                x_share(lax.rem(z + k, nz), x).start()
        if last:
            own_x.wait()
            for k in range(1, nz):
                x_share(lax.rem(z + k, nz), 1 - x).wait_recv()
            for k in range(xs.shape[0] // group):
                part = pl.ds(k * group, group)
                xt[:, part] = xs[part, :].T

        def step(c, _):
            if not last:
                for (_, zz, there), kind in zip(sources(j + 1), (UP, DOWN)):

                    def pass_on(zz=zz, kind=kind):
                        arrived(zz, q, c)
                        up_or_down(kind, zz, c)
                        send(ACROSS, zz, q, c)
                        send(TWIN, zz, q, c)

                    when(there, pass_on)
            for slot, zz, there in sources(j):

                def over(zz=zz):
                    arrived(zz, across, c)
                    send(TWIN, zz, across, c)

                when(there, over)

            if j > 0:
                @pl.when(c == 2)
                def _():
                    for slot, zz, there in sources(j - 1):
                        when(there, functools.partial(finish, slot, zz, j == 1, False))

            for slot, zz, there in sources(j):

                def use(slot=slot, zz=zz):
                    arrived(zz, twin, c)
                    arrived(zz, diagonal, c)
                    add_input(slot, zz, c)

                when(there, use)

            @pl.when(c == chunks - 1)
            def _():
                for slot, zz, there in sources(j):
                    when(there, functools.partial(exchange, slot, zz))

            if last:
                for distance in range(1, nz - 1):
                    pl.when(c == chunks - 1 - 2 * (nz - 2 - distance))(
                        functools.partial(share_from, distance)
                    )

                turn = lax.rem(c, 2)

                def out_copy(cc):
                    return pltpu.make_async_copy(
                        stage.at[turn], gw_out.at[:, columns(cc)], gw_sem.at[turn]
                    )

                @pl.when(c >= 2)
                def _():
                    out_copy(c - 2).wait()

                def piece(i, _):
                    here = pl.ds(pl.multiple_of(i * narrow, narrow), narrow)
                    there = pl.ds(pl.multiple_of(c * wide + i * narrow, narrow), narrow)
                    stage[turn, :, here] = jnp.dot(
                        xt[...], gh[:, there], preferred_element_type=F32
                    ).astype(BF16)
                    return 0

                lax.fori_loop(0, wide // narrow, piece, 0)
                out_copy(c).start()
            return 0

        lax.fori_loop(0, chunks, step, 0)

    for slot, zz, there in sources(nz - 1):
        when(there, functools.partial(finish, slot, zz, False, True))

    for k in range(nz):
        zs = lax.rem(z + k, nz)

        def settle(zs=zs, k=k):
            o_share(zs, 1 - x).wait_recv()
            o_share(zs, x).wait_send()
            if k > 0:
                o_move(zs, z).wait_send()

        pl.when((zs - z < nz - 1) & (z - zs < nz - 1))(settle)
    gi_copy = pltpu.make_async_copy(gin, gi_out, gi_sem)
    gi_copy.start()
    for k in range(1, nz):
        x_move(lax.rem(z + k, nz), z).wait_send()
        x_share(lax.rem(z + k, nz), x).wait_send()
    everything = pl.ds(0, hidden)
    for zz in range(nz):
        for there, kind in (((z < nz - 1) & (z >= zz), UP), ((z > 0) & (z <= zz), DOWN)):
            pl.when(there)(
                lambda kind=kind, zz=zz: move(kind, zz, q, everything, 0).wait_send()
            )
        move(ACROSS, zz, q, everything, 0).wait_send()
        move(TWIN, zz, q, everything, 0).wait_send()
        move(TWIN, zz, across, everything, 0).wait_send()
    for c in range(max(chunks - 2, 0), chunks):
        pltpu.make_async_copy(
            stage.at[c % 2], gw_out.at[:, pl.ds(c * wide, wide)], gw_sem.at[c % 2]
        ).wait()
    gi_copy.wait()
    for _, zz, there in sources(nz - 1):
        when(there, lambda zz=zz: pltpu.make_async_copy(osend.at[zz], far_out, far_sem).wait())


def hand_on(source, target):
    target[...] = source[...]


def handed_on(array):
    size, columns = array.shape
    part = 64 if size % 64 == 0 else size
    block = pl.BlockSpec((part, columns), lambda i: (i, 0))
    return pl.pallas_call(
        hand_on,
        grid=(size // part,),
        out_shape=jax.ShapeDtypeStruct(array.shape, array.dtype),
        in_specs=[block],
        out_specs=block,
        compiler_params=pltpu.CompilerParams(vmem_limit_bytes=60 * 1024 * 1024),
        cost_estimate=pl.CostEstimate(
            flops=0, bytes_accessed=4 * size * columns, transcendentals=0
        ),
    )(array)


def fused(nz, inputs, weight, grad_out, pre_act):
    group, model = inputs.shape
    depth, hidden = weight.shape
    rows = grad_out.shape[0]
    tokens = nz * group
    chunks = 12
    wide = hidden // chunks
    half = group // 2
    vmem = pl.BlockSpec(memory_space=pltpu.VMEM)
    hbm = pl.BlockSpec(memory_space=pl.ANY)
    dma = pltpu.SemaphoreType.DMA
    grad_in, grad_weight, far = pl.pallas_call(
        functools.partial(kernel, nz, chunks),
        out_shape=(
            jax.ShapeDtypeStruct((group, model), BF16),
            jax.ShapeDtypeStruct((depth, hidden), BF16),
            jax.ShapeDtypeStruct((half, depth), BF16),
        ),
        in_specs=[vmem, vmem, hbm, hbm],
        out_specs=(hbm, hbm, hbm),
        scratch_shapes=[
            pltpu.VMEM((tokens, hidden), BF16),
            pltpu.VMEM((depth, hidden), BF16),
            pltpu.VMEM((tokens, depth), BF16),
            pltpu.VMEM((depth, tokens), BF16),
            pltpu.VMEM((4, group, depth), F32),
            pltpu.VMEM((nz, half, depth), BF16),
            pltpu.VMEM((nz, half, depth), BF16),
            pltpu.VMEM((nz, half, depth), BF16),
            pltpu.VMEM((group, model), BF16),
            pltpu.VMEM((2, depth, wide), BF16),
            dma((4, nz, 4)),
            dma((nz, 4, chunks)),
            dma((nz, 2)),
            dma((nz, 2)),
            dma((nz,)),
            dma((nz,)),
            dma((nz, 2)),
            dma((nz, 2)),
            dma(()),
            dma((2,)),
            dma(()),
            dma(()),
        ],
        compiler_params=pltpu.CompilerParams(
            collective_id=0, has_side_effects=True, vmem_limit_bytes=62 * 1024 * 1024
        ),
        cost_estimate=pl.CostEstimate(
            flops=4 * tokens * depth * hidden,
            bytes_accessed=4 * depth * hidden,
            transcendentals=rows * hidden,
        ),
    )(grad_out, pre_act, inputs, weight)
    z, x = lax.axis_index("gx"), lax.axis_index("gy")
    end = 2 * (nz - 1)
    ours = lax.ppermute(far, "gx", [(0, nz - 1), (nz - 1, 0)])
    theirs = lax.ppermute(
        far, ("gx", "gy"), [(0, end + 1), (1, end), (end, 1), (end + 1, 0)]
    )
    grad_weight = handed_on(grad_weight)
    pair = jnp.where(
        x == 0, jnp.concatenate([ours, theirs]), jnp.concatenate([theirs, ours])
    )
    place = lax.broadcasted_iota(jnp.int32, (1, model), 1) // depth
    spread = jnp.where(jnp.abs(place - z) == nz - 1, jnp.concatenate([pair] * nz, axis=1), grad_in)
    return spread, grad_weight


def plain(inputs, weight, grad_out, pre_act):
    grad_hidden = (grad_out.astype(F32) * gelu_slope(pre_act.astype(F32))).astype(BF16)
    input_cols = lax.all_to_all(inputs, "gx", split_axis=1, concat_axis=0, tiled=True)
    piece = lax.all_gather(grad_hidden, ("gx", "gz"), axis=0, tiled=True)
    weight_sum = lax.dot_general(
        input_cols, piece, (((0,), (0,)), ((), ())), preferred_element_type=F32
    )
    product = lax.dot_general(
        piece, weight, (((1,), (1,)), ((), ())), preferred_element_type=F32
    )
    summed = lax.psum(product, "gy").astype(BF16)
    grad_in = lax.all_to_all(summed, "gx", split_axis=0, concat_axis=1, tiled=True)
    return (grad_in, weight_sum.astype(BF16))


def solution(mesh):
    in_specs = (P("gx", "gz"), P(("gz", "gx"), "gy"), P(("gx", "gz"), "gy"), P(("gx", "gz"), "gy"))
    out_specs = (P("gx", "gz"), P(("gz", "gx"), "gy"))
    if mesh.shape["gy"] == 2 and mesh.shape["gz"] == 4 and mesh.shape["gx"] > 1:
        shards = functools.partial(fused, mesh.shape["gx"])
    else:
        shards = plain
    return jax.shard_map(shards, mesh=mesh, in_specs=in_specs, out_specs=out_specs, check_vma=False)
```

```python
import functools

import jax
import jax.numpy as jnp
from jax import lax
from jax.experimental import pallas as pl
from jax.experimental.pallas import tpu as pltpu
from jax.sharding import PartitionSpec as P

MESH = pl.DeviceIdType.MESH
F32 = jnp.float32
BF16 = jnp.bfloat16
UP, DOWN, ACROSS, TWIN = 0, 1, 2, 3


def gelu_slope(value):
    scale = 0.7978845608028654
    tangent = jnp.tanh(scale * (value + 0.044715 * value * value * value))
    inner = scale * (1.0 + 3.0 * 0.044715 * value * value)
    return 0.5 * (1.0 + tangent) + 0.5 * value * (1.0 - tangent * tangent) * inner


def kernel(
    nz, chunks,
    go, pa, x_hbm, w_hbm,
    gi_out, gw_out,
    gh, w, xs, xt, acc, psend, precv, osend, gin, stage,
    ring_send, ring_recv, x_send, x_recv, p_send, p_recv, o_send, o_recv, w_sem, gw_sem, gi_sem,
):
    z, x, q = lax.axis_index("gx"), lax.axis_index("gy"), lax.axis_index("gz")
    rows = go.shape[0]
    group = 4 * rows
    half = group // 2
    hidden = gh.shape[1]
    wide = hidden // chunks
    depth = w.shape[0]
    twin = q + 1 - 2 * lax.rem(q, 2)
    across = lax.rem(q + 2, 4)
    diagonal = lax.rem(twin + 2, 4)

    def at(zz, xx, qq):
        return (zz, xx, qq)

    barrier = pltpu.get_barrier_semaphore()
    for k in range(1, nz):
        for xx in (x, 1 - x):
            pl.semaphore_signal(
                barrier, inc=1, device_id=at(lax.rem(z + k, nz), xx, q), device_id_type=MESH
            )
    for partner in (at(z, 1 - x, q), at(z, x, twin), at(z, x, across)):
        pl.semaphore_signal(barrier, inc=1, device_id=partner, device_id_type=MESH)

    w_copy = pltpu.make_async_copy(w_hbm, w, w_sem)
    w_copy.start()

    def columns(c):
        return pl.ds(pl.multiple_of(c * wide, wide), wide)

    def block(zz, qq, cols):
        return gh.at[pl.ds(pl.multiple_of(zz * group + qq * rows, rows), rows), cols]

    def partner(kind):
        return (at(z + 1, x, q), at(z - 1, x, q), at(z, x, across), at(z, x, twin))[kind]

    def move(kind, zz, qq, cols, c):
        return pltpu.make_async_remote_copy(
            src_ref=block(zz, qq, cols),
            dst_ref=block(zz, qq, cols),
            send_sem=ring_send.at[kind, zz, qq],
            recv_sem=ring_recv.at[zz, qq, c],
            device_id=partner(kind),
            device_id_type=MESH,
        )

    def send(kind, zz, qq, c):
        move(kind, zz, qq, columns(c), c).start()

    def arrived(zz, qq, c):
        move(TWIN, zz, qq, columns(c), c).wait_recv()

    def up_or_down(kind, zz, c):
        if kind == UP:
            pl.when(z < nz - 1)(lambda: send(UP, zz, q, c))
        else:
            pl.when(z > 0)(lambda: send(DOWN, zz, q, c))

    narrow = min(256, wide)

    def make_own(c, _):
        def piece(i, _):
            cols = pl.ds(pl.multiple_of(c * wide + i * narrow, narrow), narrow)
            value = go[:, cols].astype(F32) * gelu_slope(pa[:, cols].astype(F32))
            block(z, q, cols)[...] = value.astype(BF16)
            return 0

        lax.fori_loop(0, wide // narrow, piece, 0)

        @pl.when(c == 0)
        def _():
            pl.semaphore_wait(barrier, 2 * (nz - 1) + 3)

        up_or_down(UP, z, c)
        up_or_down(DOWN, z, c)
        send(ACROSS, z, q, c)
        send(TWIN, z, q, c)
        return 0

    lax.fori_loop(0, chunks, make_own, 0)
    w_copy.wait()

    def x_rows(zs, xx):
        return xs.at[pl.ds(pl.multiple_of(zs * group + xx * half, half), half), :]

    def x_move(zt, zs):
        return pltpu.make_async_remote_copy(
            src_ref=x_hbm.at[
                pl.ds(pl.multiple_of(x * half, half), half),
                pl.ds(pl.multiple_of(zt * depth, depth), depth),
            ],
            dst_ref=x_rows(zs, x),
            send_sem=x_send.at[zt, 0],
            recv_sem=x_recv.at[zs, x],
            device_id=at(zt, x, q),
            device_id_type=MESH,
        )

    def x_share(zs, xx):
        return pltpu.make_async_remote_copy(
            src_ref=x_rows(zs, xx),
            dst_ref=x_rows(zs, xx),
            send_sem=x_send.at[zs, 1],
            recv_sem=x_recv.at[zs, xx],
            device_id=at(z, 1 - x, q),
            device_id_type=MESH,
        )

    own_x = pltpu.make_async_copy(
        x_hbm.at[:, pl.ds(pl.multiple_of(z * depth, depth), depth)],
        xs.at[pl.ds(pl.multiple_of(z * group, group), group), :],
        x_recv.at[z, 0],
    )

    def sources(j):
        if j == 0:
            return [(0, z, None)]
        first = 2 * (j % 2)
        return [(first, z - j, z >= j), (first + 1, z + j, z + j < nz)]

    def when(condition, body):
        if condition is None:
            body()
        else:
            pl.when(condition)(body)

    tile = min(256, depth)

    def add_input(slot, zz, c):
        tokens = pl.ds(pl.multiple_of(zz * group, group), group)

        def piece(i, _):
            out = pl.ds(pl.multiple_of(i * tile, tile), tile)
            part = lax.dot_general(
                gh[tokens, columns(c)], w[out, columns(c)],
                (((1,), (1,)), ((), ())), preferred_element_type=F32,
            )

            @pl.when(c == 0)
            def _():
                acc[slot, :, out] = part

            @pl.when(c > 0)
            def _():
                acc[slot, :, out] += part

            return 0

        lax.fori_loop(0, depth // tile, piece, 0)

    def p_move(zz):
        return pltpu.make_async_remote_copy(
            src_ref=psend.at[zz],
            dst_ref=precv.at[zz],
            send_sem=p_send.at[zz],
            recv_sem=p_recv.at[zz],
            device_id=at(z, 1 - x, q),
            device_id_type=MESH,
        )

    def o_dst(zs, xx):
        return gin.at[
            pl.ds(pl.multiple_of(xx * half, half), half),
            pl.ds(pl.multiple_of(zs * depth, depth), depth),
        ]

    def o_move(zt, zs):
        return pltpu.make_async_remote_copy(
            src_ref=osend.at[zt],
            dst_ref=o_dst(zs, x),
            send_sem=o_send.at[zt, 0],
            recv_sem=o_recv.at[zs, x],
            device_id=at(zt, x, q),
            device_id_type=MESH,
        )

    def o_share(zs, xx):
        return pltpu.make_async_remote_copy(
            src_ref=o_dst(zs, xx),
            dst_ref=o_dst(zs, xx),
            send_sem=o_send.at[zs, 1],
            recv_sem=o_recv.at[zs, xx],
            device_id=at(z, 1 - x, q),
            device_id_type=MESH,
        )

    def share_from(distance):
        for zs, there in ((z - distance, z >= distance), (z + distance, z + distance < nz)):

            def pass_over(zs=zs):
                o_move(z, zs).wait_recv()
                o_share(zs, x).start()

            pl.when(there)(pass_over)

    def exchange(slot, zz):
        theirs = pl.ds(pl.multiple_of((1 - x) * half, half), half)
        psend[zz] = acc[slot, theirs, :].astype(BF16)
        p_move(zz).start()

    def finish(slot, zz, own):
        ours = pl.ds(pl.multiple_of(x * half, half), half)
        p_move(zz).wait()
        osend[zz] = (acc[slot, ours, :] + precv[zz].astype(F32)).astype(BF16)
        if own:
            o_dst(z, x)[...] = osend[zz]
            o_share(z, x).start()
        else:
            o_move(zz, z).start()

    for j in range(nz):
        last = j == nz - 1
        if j == 1:
            own_x.start()
            for k in range(1, nz):
                x_move(lax.rem(z + k, nz), z).start()
        if j == max(nz - 2, 1):
            for k in range(1, nz):
                x_move(z, lax.rem(z + k, nz)).wait_recv()
                x_share(lax.rem(z + k, nz), x).start()
        if last:
            own_x.wait()
            for k in range(1, nz):
                x_share(lax.rem(z + k, nz), 1 - x).wait_recv()
            for k in range(xs.shape[0] // group):
                part = pl.ds(k * group, group)
                xt[:, part] = xs[part, :].T

        def step(c, _):
            if not last:
                for (_, zz, there), kind in zip(sources(j + 1), (UP, DOWN)):

                    def pass_on(zz=zz, kind=kind):
                        arrived(zz, q, c)
                        up_or_down(kind, zz, c)
                        send(ACROSS, zz, q, c)
                        send(TWIN, zz, q, c)

                    when(there, pass_on)
            for slot, zz, there in sources(j):

                def over(zz=zz):
                    arrived(zz, across, c)
                    send(TWIN, zz, across, c)

                when(there, over)

            if j > 0:
                @pl.when(c == 2)
                def _():
                    for slot, zz, there in sources(j - 1):
                        when(there, functools.partial(finish, slot, zz, j == 1))

            for slot, zz, there in sources(j):

                def use(slot=slot, zz=zz):
                    arrived(zz, twin, c)
                    arrived(zz, diagonal, c)
                    add_input(slot, zz, c)

                when(there, use)

            @pl.when(c == chunks - 1)
            def _():
                for slot, zz, there in sources(j):
                    when(there, functools.partial(exchange, slot, zz))

            if last:
                for distance in range(1, nz - 1):
                    pl.when(c == chunks - 1 - 2 * (nz - 2 - distance))(
                        functools.partial(share_from, distance)
                    )

                turn = lax.rem(c, 2)

                def out_copy(cc):
                    return pltpu.make_async_copy(
                        stage.at[turn], gw_out.at[:, columns(cc)], gw_sem.at[turn]
                    )

                @pl.when(c >= 2)
                def _():
                    out_copy(c - 2).wait()

                def piece(i, _):
                    here = pl.ds(pl.multiple_of(i * narrow, narrow), narrow)
                    there = pl.ds(pl.multiple_of(c * wide + i * narrow, narrow), narrow)
                    stage[turn, :, here] = jnp.dot(
                        xt[...], gh[:, there], preferred_element_type=F32
                    ).astype(BF16)
                    return 0

                lax.fori_loop(0, wide // narrow, piece, 0)
                out_copy(c).start()
            return 0

        lax.fori_loop(0, chunks, step, 0)

    for slot, zz, there in sources(nz - 1):
        when(there, functools.partial(finish, slot, zz, nz == 1))

    share_from(nz - 1)
    for k in range(nz):
        zs = lax.rem(z + k, nz)
        o_share(zs, 1 - x).wait_recv()
        o_share(zs, x).wait_send()
        if k > 0:
            o_move(zs, z).wait_send()
    gi_copy = pltpu.make_async_copy(gin, gi_out, gi_sem)
    gi_copy.start()
    for k in range(1, nz):
        x_move(lax.rem(z + k, nz), z).wait_send()
        x_share(lax.rem(z + k, nz), x).wait_send()
    everything = pl.ds(0, hidden)
    for zz in range(nz):
        for there, kind in (((z < nz - 1) & (z >= zz), UP), ((z > 0) & (z <= zz), DOWN)):
            pl.when(there)(
                lambda kind=kind, zz=zz: move(kind, zz, q, everything, 0).wait_send()
            )
        move(ACROSS, zz, q, everything, 0).wait_send()
        move(TWIN, zz, q, everything, 0).wait_send()
        move(TWIN, zz, across, everything, 0).wait_send()
    for c in range(max(chunks - 2, 0), chunks):
        pltpu.make_async_copy(
            stage.at[c % 2], gw_out.at[:, pl.ds(c * wide, wide)], gw_sem.at[c % 2]
        ).wait()
    gi_copy.wait()


def fused(nz, inputs, weight, grad_out, pre_act):
    group, model = inputs.shape
    depth, hidden = weight.shape
    rows = grad_out.shape[0]
    tokens = nz * group
    chunks = 16
    wide = hidden // chunks
    half = group // 2
    vmem = pl.BlockSpec(memory_space=pltpu.VMEM)
    hbm = pl.BlockSpec(memory_space=pl.ANY)
    dma = pltpu.SemaphoreType.DMA
    return pl.pallas_call(
        functools.partial(kernel, nz, chunks),
        out_shape=(
            jax.ShapeDtypeStruct((group, model), BF16),
            jax.ShapeDtypeStruct((depth, hidden), BF16),
        ),
        in_specs=[vmem, vmem, hbm, hbm],
        out_specs=(hbm, hbm),
        scratch_shapes=[
            pltpu.VMEM((tokens, hidden), BF16),
            pltpu.VMEM((depth, hidden), BF16),
            pltpu.VMEM((tokens, depth), BF16),
            pltpu.VMEM((depth, tokens), BF16),
            pltpu.VMEM((4, group, depth), F32),
            pltpu.VMEM((nz, half, depth), BF16),
            pltpu.VMEM((nz, half, depth), BF16),
            pltpu.VMEM((nz, half, depth), BF16),
            pltpu.VMEM((group, model), BF16),
            pltpu.VMEM((2, depth, wide), BF16),
            dma((4, nz, 4)),
            dma((nz, 4, chunks)),
            dma((nz, 2)),
            dma((nz, 2)),
            dma((nz,)),
            dma((nz,)),
            dma((nz, 2)),
            dma((nz, 2)),
            dma(()),
            dma((2,)),
            dma(()),
        ],
        compiler_params=pltpu.CompilerParams(
            collective_id=0, has_side_effects=True, vmem_limit_bytes=62 * 1024 * 1024
        ),
        cost_estimate=pl.CostEstimate(
            flops=4 * tokens * depth * hidden,
            bytes_accessed=4 * depth * hidden,
            transcendentals=rows * hidden,
        ),
    )(grad_out, pre_act, inputs, weight)


def plain(inputs, weight, grad_out, pre_act):
    grad_hidden = (grad_out.astype(F32) * gelu_slope(pre_act.astype(F32))).astype(BF16)
    input_cols = lax.all_to_all(inputs, "gx", split_axis=1, concat_axis=0, tiled=True)
    piece = lax.all_gather(grad_hidden, ("gx", "gz"), axis=0, tiled=True)
    weight_sum = lax.dot_general(
        input_cols, piece, (((0,), (0,)), ((), ())), preferred_element_type=F32
    )
    product = lax.dot_general(
        piece, weight, (((1,), (1,)), ((), ())), preferred_element_type=F32
    )
    summed = lax.psum(product, "gy").astype(BF16)
    grad_in = lax.all_to_all(summed, "gx", split_axis=0, concat_axis=1, tiled=True)
    return (grad_in, weight_sum.astype(BF16))


def solution(mesh):
    in_specs = (P("gx", "gz"), P(("gz", "gx"), "gy"), P(("gx", "gz"), "gy"), P(("gx", "gz"), "gy"))
    out_specs = (P("gx", "gz"), P(("gz", "gx"), "gy"))
    if mesh.shape["gy"] == 2 and mesh.shape["gz"] == 4 and mesh.shape["gx"] > 1:
        shards = functools.partial(fused, mesh.shape["gx"])
    else:
        shards = plain
    return jax.shard_map(shards, mesh=mesh, in_specs=in_specs, out_specs=out_specs, check_vma=False)
```
